256 devices in a mesh: ctx: 16 (over y, z_hi), head: 4 (over z_lo, core), dp: 4 (over x).
Axes of the slice: x: 4, y: 4, z: 8 (z_hi: 4, z_lo: 2; z = z_hi * 2 + z_lo), core: 2. Of those that a mesh axis runs over, the one named last changes fastest.
Arguments:
- query_rows: bfloat16 [32768, 4096], P(('dp', 'ctx', 'head')), parts along dimension 0, may hold values from -6 to 6
- key_rows: bfloat16 [32768, 512], P(('dp', 'ctx', 'head')), parts along dimension 0, may hold values from -6 to 6
- value_rows: bfloat16 [32768, 512], P(('dp', 'ctx', 'head')), parts along dimension 0, may hold values from -6 to 6
- fwd_output: bfloat16 [32768, 4096], P(('dp', 'ctx', 'head')), parts along dimension 0, may hold values from -6 to 6
- grad_output: bfloat16 [32768, 4096], P(('dp', 'ctx', 'head')), parts along dimension 0, may hold values from -6 to 6
- log_normalizer: float32 [32768, 32], P(('dp', 'ctx', 'head')), parts along dimension 0, may hold values from -1 to 12
- doc_lengths: int32 [24], P('dp'), parts along dimension 0, may hold values from 256 to 2048, as said below
Outputs:
- grad_query: bfloat16 [32768, 4096], P(('dp', 'ctx', 'head')), parts along dimension 0
- grad_key: bfloat16 [32768, 512], P(('dp', 'ctx', 'head')), parts along dimension 0
- grad_value: bfloat16 [32768, 512], P(('dp', 'ctx', 'head')), parts along dimension 0
The draws below stay inside these ranges and needn't reach their ends.
There are 4 independent parts, one for each index of `dp`. The reference program is written for one: setup_inputs(seed, part) draws one part's arguments, and reference() takes and returns one part's arrays. A program takes and returns all parts, laid end to end along the dimension named above; each array names one. Nothing has to cross between parts.
Inputs may be any that keep to these rules, and one draw needn't show every extreme that they name: `doc_lengths`: the 6 lengths sum to 8192; the largest is exactly 2048.
All inputs are finite; a program needn't handle non-finite values.
Results may differ from the reference program's by a relative error of at most 0.0053.
Values may be sent and summed in bfloat16 or wider, within the bound.
A program may use at most 64 MiB of HBM per device.

```python
import jax
import jax.numpy as jnp
from jax import lax

HEADS = 32
KV_HEADS = 4
HD = 128
DOCS = 6
SEQ = 8192


def shared_lengths(key):
    key = jax.random.fold_in(key, 101)
    place_key, weight_key = jax.random.split(key)
    shortest = SEQ // 32
    others = DOCS - 1
    spread = SEQ - SEQ // 4 - others * shortest
    weights = jax.random.randint(weight_key, (others,), 500, 1000)
    shares = weights * spread // jnp.sum(weights)
    shares = shares.at[0].add(spread - jnp.sum(shares))
    smaller = shortest + shares
    place = jax.random.randint(place_key, (), 0, DOCS)
    slots = jnp.arange(DOCS)
    picked = jnp.clip(slots - (slots > place).astype(jnp.int32), 0, others - 1)
    return jnp.where(slots == place, SEQ // 4, smaller[picked]).astype(jnp.int32)


def draw_doc_lengths(key, part):
    return shared_lengths(key)


def draw_log_normalizer(key, part):
    lengths = shared_lengths(key)
    key = jax.random.fold_in(key, 7)
    doc_ends = jnp.cumsum(lengths)
    doc_starts = doc_ends - lengths
    positions = jnp.arange(SEQ)
    doc_ids = jnp.sum((positions[:, None] >= doc_ends[None, :]).astype(jnp.int32), axis=1)
    offsets = (positions - doc_starts[doc_ids]).astype(jnp.float32)
    base_level = jnp.log(offsets + 1.0) + 0.5
    noise = 0.3 * jnp.clip(jax.random.normal(key, (SEQ, HEADS)), -3.0, 3.0)
    return (base_level[:, None] + noise).astype(jnp.float32)


def levels(key, shape, cuts, least, largest):
    def one(axis_at, blocks):
        steps = jax.random.uniform(jax.random.fold_in(jax.random.fold_in(key, 6), axis_at), (blocks,), jnp.float32, least / len(cuts), largest / len(cuts))
        return jnp.repeat(jnp.exp(steps), shape[axis_at] // blocks).reshape((-1,) + (1,) * (len(shape) - axis_at - 1))

    loudness = one(*cuts[0])
    for cut in cuts[1:]:
        loudness = loudness * one(*cut)
    return loudness


def bell_draw(key, shape, scale, bound, shards=(), kind=jnp.bfloat16):
    level = levels(key, shape, shards, -0.22, 0.18) if shards else 1.0
    array = jax.random.normal(key, shape, jnp.float32) * scale * level
    return jnp.minimum(jnp.maximum(array, -bound), bound).astype(kind)


def setup_inputs(seed: int = 0, part: int = 0) -> dict:
    seeds = jax.random.split(jax.random.key(seed), 8)
    part_keys = jax.random.split(jax.random.fold_in(seeds[7], part), 8)
    query_rows = bell_draw(part_keys[0], (SEQ, HEADS * HD), 1.0, 6.0, ((0, 64),))
    key_rows = bell_draw(part_keys[1], (SEQ, KV_HEADS * HD), 1.0, 6.0, ((0, 64),))
    value_rows = bell_draw(part_keys[2], (SEQ, KV_HEADS * HD), 1.0, 6.0, ((0, 64),))
    fwd_output = bell_draw(part_keys[3], (SEQ, HEADS * HD), 1.0, 6.0, ((0, 64),))
    grad_output = bell_draw(part_keys[4], (SEQ, HEADS * HD), 1.0, 6.0, ((0, 64),))
    log_normalizer = draw_log_normalizer(jax.random.fold_in(jax.random.fold_in(seeds[7], part), 71), part)
    doc_lengths = draw_doc_lengths(jax.random.fold_in(jax.random.fold_in(seeds[7], part), 71), part)
    return dict(query_rows=query_rows, key_rows=key_rows, value_rows=value_rows, fwd_output=fwd_output, grad_output=grad_output, log_normalizer=log_normalizer, doc_lengths=doc_lengths)


def reference(query_rows, key_rows, value_rows, fwd_output, grad_output, log_normalizer, doc_lengths):
    length = query_rows.shape[0]
    group = HEADS // KV_HEADS
    score_scale = HD ** -0.5
    doc_ends = jnp.cumsum(doc_lengths).astype(jnp.int32)
    positions = jnp.arange(length, dtype=jnp.int32)
    doc_ids = jnp.sum((positions[:, None] >= doc_ends[None, :]).astype(jnp.int32), axis=1)
    allowed = (positions[None, :] <= positions[:, None]) & (doc_ids[None, :] == doc_ids[:, None])
    delta = jnp.sum((fwd_output.astype(jnp.float32) * grad_output.astype(jnp.float32)).reshape(length, HEADS, HD), axis=-1)
    query_heads = query_rows.reshape(length, HEADS, HD).transpose(1, 0, 2)
    grad_heads = grad_output.reshape(length, HEADS, HD).transpose(1, 0, 2)
    key_heads = key_rows.reshape(length, KV_HEADS, HD).transpose(1, 0, 2)
    value_heads = value_rows.reshape(length, KV_HEADS, HD).transpose(1, 0, 2)
    group_index = (jnp.arange(HEADS, dtype=jnp.int32) // group).astype(jnp.int32)

    def one_head(items):
        head_query, head_grad, head_norm, head_delta, kv_index = items
        head_key = key_heads[kv_index]
        head_value = value_heads[kv_index]
        scores = jnp.dot(head_query, head_key.T, preferred_element_type=jnp.float32) * score_scale
        probs = jnp.where(allowed, jnp.exp(scores - head_norm[:, None]), 0.0)
        probs_half = probs.astype(jnp.bfloat16)
        value_term = jnp.dot(probs_half.T, head_grad, preferred_element_type=jnp.float32)
        grad_probs = jnp.dot(head_grad, head_value.T, preferred_element_type=jnp.float32)
        grad_scores = (probs * (grad_probs - head_delta[:, None])).astype(jnp.bfloat16)
        query_term = jnp.dot(grad_scores, head_key, preferred_element_type=jnp.float32) * score_scale
        key_term = jnp.dot(grad_scores.T, head_query, preferred_element_type=jnp.float32) * score_scale
        return query_term, key_term, value_term

    query_terms, key_terms, value_terms = lax.map(one_head, (query_heads, grad_heads, log_normalizer.T, delta.T, group_index))
    grad_query = query_terms.transpose(1, 0, 2).reshape(length, HEADS * HD).astype(jnp.bfloat16)
    key_sum = key_terms.reshape(KV_HEADS, group, length, HD).sum(axis=1)
    value_sum = value_terms.reshape(KV_HEADS, group, length, HD).sum(axis=1)
    grad_key = key_sum.transpose(1, 0, 2).reshape(length, KV_HEADS * HD).astype(jnp.bfloat16)
    grad_value = value_sum.transpose(1, 0, 2).reshape(length, KV_HEADS * HD).astype(jnp.bfloat16)
    return (grad_query, grad_key, grad_value)
```

```python
import functools

import jax
import jax.numpy as jnp
from jax import lax
from jax.experimental import pallas as pl
from jax.experimental.pallas import tpu as pltpu
from jax.sharding import PartitionSpec as P

HD = 128
LOG2E = 1.4426950408889634
SCALE = HD ** (-0.5)
HOPS = 8
MASKED = -1e30
MESH = pl.DeviceIdType.MESH
NN = (((1,), (0,)), ((), ()))
NT = (((1,), (1,)), ((), ()))
BF = jnp.bfloat16
F32 = jnp.float32


def dot(a, b, dims):
    return lax.dot_general(a, b, dims, preferred_element_type=F32)


def kernel(
    chips, group, rows, parts,
    q_hbm, k_hbm, v_hbm, o_hbm, do_hbm, lse_ref, len_ref,
    dq_hbm, dk_ref, dv_ref,
    qs, dos, qt, dot_t, o_nat, do_nat, lb, db, lo_ref, pd, dqacc, dqs,
    kv, acc, pf, p8, own, h8, home,
    fh_send, fh_recv, ring_send, ring_recv, acc_send, acc_recv,
    home_send, home_recv, h8_send, h8_recv, own_send, own_recv,
    nat_sem, q_loc, q_send, q_recv, pd_send, pd_recv, dq_loc, dq_send, dq_recv,
):
    heads = 2 * group
    block = 2 * rows
    at_ctx, at_head = lax.axis_index("ctx"), lax.axis_index("head")
    core = lax.rem(at_head, 2)
    chip = at_ctx * 2 + lax.div(at_head, 2)
    other = 1 - core

    def device(hop, to_core):
        to = lax.rem(chip + hop + chips, chips)
        return {"ctx": lax.div(to, 2), "head": lax.rem(to, 2) * 2 + to_core}

    def remote(src, dst, ss, rs, hop, to_core):
        return pltpu.make_async_remote_copy(
            src_ref=src, dst_ref=dst, send_sem=ss, recv_sem=rs,
            device_id=device(hop, to_core), device_id_type=MESH,
        )

    def cols(head, width=1):
        return pl.ds(pl.multiple_of(head * HD, HD), width * HD)

    def half(which):
        return pl.ds(pl.multiple_of(which * rows, rows), rows)

    barrier = pltpu.get_barrier_semaphore()
    partners = [(0, other)] + [(h, c) for h in (1, -1, 7, -7, 8, -8) for c in (0, 1)]
    for hop, c in partners:
        pl.semaphore_signal(barrier, inc=1, device_id=device(hop, c), device_id_type=MESH)
    nat = [
        pltpu.make_async_copy(o_hbm, o_nat, nat_sem.at[0]),
        pltpu.make_async_copy(do_hbm, do_nat, nat_sem.at[1]),
    ]
    for cp in nat:
        cp.start()
    pl.semaphore_wait(barrier, len(partners))

    kinds = [(0, 0, 1, 1), (1, 1, 1, 7), (2, 0, 0, 0), (3, 1, 8, 0), (4, 0, 8, 8), (5, 1, 0, 8)]

    def first(kind, d, which):
        _, b, slot, hop = kinds[kind]
        to_core = core if d == 0 else other
        src = (k_hbm, v_hbm)[which].at[:, cols(2 * to_core + b)]
        dst = kv.at[b, slot, which, half(core)]
        if hop == 0 and d == 0:
            return pltpu.make_async_copy(src, dst, fh_recv.at[kind, core, which])
        return remote(src, dst, fh_send.at[kind, d, which], fh_recv.at[kind, core, which], hop, to_core)

    def start_first(kind):
        for which in (0, 1):
            for d in (0, 1):
                first(kind, d, which).start()

    def wait_first(kind, which):
        _, b, slot, hop = kinds[kind]
        for c in (0, 1):
            dst = kv.at[b, slot, which, pl.ds(c * rows, rows)]
            pltpu.make_async_copy(dst, dst, fh_recv.at[kind, c, which]).wait()

    start_first(0)
    start_first(1)

    @pl.loop(0, heads)
    def _(h):
        for i, (src, dst) in enumerate(((q_hbm, qs), (do_hbm, dos))):
            pltpu.make_async_copy(
                src.at[:, cols(heads * core + h)], dst.at[h, half(core)], q_loc.at[i]
            ).start()
            remote(
                src.at[:, cols(heads * other + h)], dst.at[h, half(core)],
                q_send.at[i], q_recv.at[i], 0, other,
            ).start()

    for kind in (2, 3, 5, 4):
        start_first(kind)

    for cp in nat:
        cp.wait()
    lane = lax.broadcasted_iota(jnp.int32, (rows, 4 * group), 1)
    delta = jnp.zeros((rows, 4 * group), F32)
    for h in range(4 * group):
        at = slice(h * HD, (h + 1) * HD)
        col = jnp.sum(o_nat[:, at].astype(F32) * do_nat[:, at].astype(F32), axis=1, keepdims=True)
        delta = jnp.where(lane == h, col, delta)
    norm = lse_ref[...] * LOG2E
    first_half = core == 0
    for i, flip in ((0, False), (1, True)):
        low = jnp.logical_xor(first_half, flip)
        pd[i, :, :heads] = jnp.where(low, norm[:, :heads], norm[:, heads:])
        pd[i, :, heads : 2 * heads] = jnp.where(low, delta[:, :heads], delta[:, heads:])
    pd_copy = remote(pd.at[1], pd.at[2], pd_send.at[0], pd_recv.at[0], 0, other)
    pd_copy.start()

    row = chip * block + lax.broadcasted_iota(jnp.int32, (block, HD), 0)
    low_key = jnp.zeros((block, HD), jnp.int32)
    end = jnp.int32(0)
    for d in range(len_ref.shape[0]):
        end = end + len_ref[d]
        low_key = jnp.where(row >= end, end, low_key)
    lo_ref[...] = low_key

    dqacc[...] = jnp.zeros_like(dqacc)
    for b in (0, 1):
        acc[b, 1] = jnp.zeros(acc.shape[2:], acc.dtype)

    for i, dst in enumerate((qs, dos)):
        mine = dst.at[:, half(core)]
        theirs = dst.at[:, half(other)]
        pltpu.make_async_copy(mine, mine, q_loc.at[i]).wait()
        pltpu.make_async_copy(theirs, theirs, q_recv.at[i]).wait()
    for h in range(heads):
        at = slice(h * block, (h + 1) * block)
        qt[:, at] = qs[h].T
        dot_t[:, at] = dos[h].T
    pd_copy.wait_recv()
    for i, at in ((0, core), (2, other)):
        for h in range(heads):
            lb[h, half(at)] = jnp.broadcast_to(pd[i, :, h : h + 1], (rows, HD))
            db[h, half(at)] = jnp.broadcast_to(pd[i, :, heads + h : heads + h + 1], (rows, HD))

    def ring(b, t, which):
        return remote(
            kv.at[b, t, which], kv.at[b, t + 1, which],
            ring_send.at[b, t, which], ring_recv.at[b, t + 1, which], 1 - 2 * b, core,
        )

    def pass_on(b, t, which):
        return remote(
            acc.at[b, t, which], acc.at[b, t + 1, which],
            acc_send.at[b, t, which], acc_recv.at[b, t + 1, which], 1 - 2 * b, core,
        )

    def go_home(b, which, r):
        return remote(
            acc.at[b, HOPS - 1, which, pl.ds(r * rows, rows)], home.at[b, core, which],
            home_send.at[b, r, which], home_recv.at[b, core, which], -7 if b == 0 else -1, r,
        )

    def far_home(b, which, r):
        return remote(
            p8.at[b, which, pl.ds(r * rows, rows)], h8.at[b, core, which],
            h8_send.at[b, r, which], h8_recv.at[b, core, which], -8, r,
        )

    def own_home(b, which):
        return remote(
            pf.at[b, which, half(other)], own.at[b, core, which],
            own_send.at[b, which], own_recv.at[b, which], 0, other,
        )

    def chunk(b, slot, distance):
        keys = kv[b, slot, 0]
        values = kv[b, slot, 1]
        key_at = (chip - distance) * block + lax.broadcasted_iota(jnp.int32, (block, block), 1)
        row_at = chip * block + lax.broadcasted_iota(jnp.int32, (block, block), 0)
        low = jnp.concatenate([lo_ref[...]] * (block // HD), axis=1) if block >= HD else lo_ref[:, :block]
        bias = jnp.where((key_at >= low) & (key_at <= row_at), 0.0, MASKED)
        dk_t = jnp.zeros((HD, block), F32)
        dv_t = jnp.zeros((HD, block), F32)
        step = min(4, group)
        for h in range(b * group, (b + 1) * group, step):
            some = slice(h, h + step)
            flat = slice(h * block, (h + step) * block)

            def wide(ref):
                x = ref[some]
                return jnp.concatenate([x] * (block // HD), axis=2) if block >= HD else x[:, :, :block]

            q = qs[some].reshape(step * block, HD)
            g = dos[some].reshape(step * block, HD)
            s = dot(q, keys, NT).reshape(step, block, block)
            dp = dot(g, values, NT).reshape(step, block, block)
            p = jnp.exp2(s * (SCALE * LOG2E) - wide(lb) + bias[None])
            ds = (p * (dp - wide(db))).astype(BF).reshape(step * block, block)
            ph = p.astype(BF).reshape(step * block, block)
            dv_t = dv_t + dot(dot_t[:, flat], ph, NN)
            dk_t = dk_t + dot(qt[:, flat], ds, NN)
            dqacc[some] += dot(ds, keys, NN).reshape(step, block, HD)
        pf[b, 0] = dk_t.T
        pf[b, 1] = dv_t.T

    for which in (0, 1):
        for b in (0, 1):
            wait_first(b, which)
            ring(b, 1, which).start()

    for b in (0, 1):
        for which in (0, 1):
            wait_first(2 + b, which)
        chunk(b, HOPS * b, 0)
        for which in (0, 1):
            own_home(b, which).start()
            own[b, core, which] = pf[b, which, half(core)]
    for b in (0, 1):
        for which in (0, 1):
            own_home(b, which).wait_send()

    @pl.loop(1, HOPS)
    def _(t):
        chunk(0, t, t)
        chunk(1, t, HOPS - t)

        @pl.when(t < HOPS - 1)
        def _():
            for which in (0, 1):
                for b in (0, 1):
                    ring(b, t, which).wait_recv()

                    @pl.when(t + 1 < HOPS - 1)
                    def _():
                        ring(b, t + 1, which).start()

        for b in (0, 1):
            for which in (0, 1):
                @pl.when(t > 1)
                def _():
                    pass_on(b, t - 1, which).wait_recv()

                acc[b, t, which] = (acc[b, t, which].astype(F32) + pf[b, which]).astype(BF)

                @pl.when(t < HOPS - 1)
                def _():
                    pass_on(b, t, which).start()

                @pl.when(t == HOPS - 1)
                def _():
                    for r in (0, 1):
                        go_home(b, which, r).start()

        @pl.when(t == 2)
        def _():
            for b in (0, 1):
                for which in (0, 1):
                    wait_first(4 + b, which)
                chunk(b, HOPS * (1 - b), HOPS)
                for which in (0, 1):
                    p8[b, which] = pf[b, which].astype(BF)
                    for r in (0, 1):
                        far_home(b, which, r).start()

    dqs[...] = (dqacc[...] * SCALE).astype(BF)

    @pl.loop(0, heads)
    def _(h):
        pltpu.make_async_copy(
            dqs.at[h, half(core)], dq_hbm.at[:, cols(heads * core + h)], dq_loc.at[0]
        ).start()
        remote(
            dqs.at[h, half(other)], dq_hbm.at[:, cols(heads * core + h)],
            dq_send.at[0], dq_recv.at[0], 0, other,
        ).start()

    for b in (0, 1):
        for which in (0, 1):
            got = own.at[b, other, which]
            pltpu.make_async_copy(got, got, own_recv.at[b, which]).wait()
            for c in (0, 1):
                for buf, sems in ((h8, h8_recv), (home, home_recv)):
                    got = buf.at[b, c, which]
                    pltpu.make_async_copy(got, got, sems.at[b, c, which]).wait()
    for c in (0, 1):
        for b in (0, 1):
            at = slice((2 * c + b) * HD, (2 * c + b + 1) * HD)
            total = [
                own[b, c, which] + h8[b, c, which].astype(F32) + home[b, c, which].astype(F32)
                for which in (0, 1)
            ]
            dk_ref[:, at] = (total[0] * SCALE).astype(BF)
            dv_ref[:, at] = total[1].astype(BF)

    for i, dst in enumerate((qs, dos)):
        out = dst.at[:, half(core)]
        pltpu.make_async_copy(out, out, q_send.at[i]).wait()
    pd_copy.wait_send()
    for kind in range(6):
        for which in (0, 1):
            for d in (0, 1):
                if not (kinds[kind][3] == 0 and d == 0):
                    first(kind, d, which).wait_send()
    for b in (0, 1):
        for which in (0, 1):
            for r in (0, 1):
                far_home(b, which, r).wait_send()
                go_home(b, which, r).wait_send()
            for t in range(1, HOPS - 1):
                ring(b, t, which).wait_send()
                pass_on(b, t, which).wait_send()
    out = dq_hbm.at[:, cols(heads * core, heads)]
    pltpu.make_async_copy(out, out, dq_loc.at[0]).wait()
    pltpu.make_async_copy(out, out, dq_send.at[0]).wait()
    got = dq_hbm.at[:, cols(heads * other, heads)]
    pltpu.make_async_copy(got, got, dq_recv.at[0]).wait()


def body(query_rows, key_rows, value_rows, fwd_output, grad_output, log_normalizer, doc_lengths):
    rows = query_rows.shape[0]
    group = query_rows.shape[1] // key_rows.shape[1]
    chips = lax.axis_size("ctx") * 2
    heads = 2 * group
    block = 2 * rows
    any_space = pl.BlockSpec(memory_space=pl.ANY)
    vmem = pl.BlockSpec(memory_space=pltpu.VMEM)
    smem = pl.BlockSpec(memory_space=pltpu.SMEM)
    dma = pltpu.SemaphoreType.DMA
    slots = HOPS + 1
    flops = 2 * slots * group * block * block * HD * 2 * 5
    return pl.pallas_call(
        functools.partial(kernel, chips, group, rows, None),
        out_shape=[
            jax.ShapeDtypeStruct(query_rows.shape, BF),
            jax.ShapeDtypeStruct(key_rows.shape, BF),
            jax.ShapeDtypeStruct(value_rows.shape, BF),
        ],
        in_specs=[any_space] * 5 + [vmem, smem],
        out_specs=[any_space, vmem, vmem],
        scratch_shapes=[
            pltpu.VMEM((heads, block, HD), BF),
            pltpu.VMEM((heads, block, HD), BF),
            pltpu.VMEM((HD, heads * block), BF),
            pltpu.VMEM((HD, heads * block), BF),
            pltpu.VMEM((rows, 2 * heads * HD), BF),
            pltpu.VMEM((rows, 2 * heads * HD), BF),
            pltpu.VMEM((heads, block, HD), F32),
            pltpu.VMEM((heads, block, HD), F32),
            pltpu.VMEM((block, HD), jnp.int32),
            pltpu.VMEM((3, rows, HD), F32),
            pltpu.VMEM((heads, block, HD), F32),
            pltpu.VMEM((heads, block, HD), BF),
            pltpu.VMEM((2, slots, 2, block, HD), BF),
            pltpu.VMEM((2, HOPS, 2, block, HD), BF),
            pltpu.VMEM((2, 2, block, HD), F32),
            pltpu.VMEM((2, 2, block, HD), BF),
            pltpu.VMEM((2, 2, 2, rows, HD), F32),
            pltpu.VMEM((2, 2, 2, rows, HD), BF),
            pltpu.VMEM((2, 2, 2, rows, HD), BF),
            dma((6, 2, 2)), dma((6, 2, 2)),
            dma((2, slots, 2)), dma((2, slots, 2)),
            dma((2, slots, 2)), dma((2, slots, 2)),
            dma((2, 2, 2)), dma((2, 2, 2)),
            dma((2, 2, 2)), dma((2, 2, 2)),
            dma((2, 2)), dma((2, 2)),
            dma((2,)), dma((2,)), dma((2,)), dma((2,)),
            dma((1,)), dma((1,)), dma((1,)), dma((1,)), dma((1,)),
        ],
        compiler_params=pltpu.CompilerParams(
            collective_id=0, has_side_effects=True, vmem_limit_bytes=56 * 2**20
        ),
        cost_estimate=pl.CostEstimate(
            flops=flops, bytes_accessed=8 * rows * 2 * heads * HD, transcendentals=flops // (10 * HD)
        ),
    )(query_rows, key_rows, value_rows, fwd_output, grad_output, log_normalizer, doc_lengths)


def solution(mesh):
    tokens = P(("dp", "ctx", "head"), None)
    return jax.shard_map(
        body,
        mesh=mesh,
        in_specs=(tokens,) * 6 + (P("dp"),),
        out_specs=(tokens,) * 3,
        check_vma=False,
    )
```

```python
import functools

import jax
import jax.numpy as jnp
from jax import lax
from jax.experimental import pallas as pl
from jax.experimental.pallas import tpu as pltpu
from jax.sharding import PartitionSpec as P

HD = 128
LOG2E = 1.4426950408889634
SCALE = HD ** (-0.5)
HOPS = 8
MASKED = -1e30
MESH = pl.DeviceIdType.MESH
NN = (((1,), (0,)), ((), ()))
NT = (((1,), (1,)), ((), ()))
BF = jnp.bfloat16
F32 = jnp.float32


def dot(a, b, dims):
    return lax.dot_general(a, b, dims, preferred_element_type=F32)


def kernel(
    chips, group, rows, parts,
    q_hbm, k_hbm, v_hbm, o_hbm, do_hbm, lse_hbm, len_hbm,
    dq_hbm, dk_ref, dv_ref,
    lse_ref, len_ref,
    qs, dos, qt, dot_t, o_nat, do_nat, lb, db, lo_ref, pd, dqacc, dqs,
    kv, acc, pf, p8, own, h8, home, relay, sums,
    fh_send, fh_recv, ring_send, ring_recv, acc_send, acc_recv,
    home_send, home_recv, h8_send, h8_recv, own_send, own_recv,
    relay_send, relay_recv, nat_sem, q_loc, q_send, q_recv, pd_send, pd_recv, dq_loc, dq_send, dq_recv,
):
    heads = 2 * group
    block = 2 * rows
    at_ctx, at_head = lax.axis_index("ctx"), lax.axis_index("head")
    core = lax.rem(at_head, 2)
    chip = at_ctx * 2 + lax.div(at_head, 2)
    other = 1 - core
    place = lax.rem(chip, HOPS)

    def device(hop, to_core):
        to = lax.rem(chip + hop + chips, chips)
        return {"ctx": lax.div(to, 2), "head": lax.rem(to, 2) * 2 + to_core}

    def remote(src, dst, ss, rs, hop, to_core):
        return pltpu.make_async_remote_copy(
            src_ref=src, dst_ref=dst, send_sem=ss, recv_sem=rs,
            device_id=device(hop, to_core), device_id_type=MESH,
        )

    def cols(head, width=1):
        return pl.ds(pl.multiple_of(head * HD, HD), width * HD)

    def half(which):
        return pl.ds(pl.multiple_of(which * rows, rows), rows)

    barrier = pltpu.get_barrier_semaphore()
    partners = [(0, other)] + [(h, c) for h in (1, -1, 7, -7, 8, -8) for c in (0, 1)]
    for hop, c in partners:
        pl.semaphore_signal(barrier, inc=1, device_id=device(hop, c), device_id_type=MESH)
    nat = [
        pltpu.make_async_copy(o_hbm, o_nat, nat_sem.at[0]),
        pltpu.make_async_copy(do_hbm, do_nat, nat_sem.at[1]),
        pltpu.make_async_copy(lse_hbm, lse_ref, nat_sem.at[2]),
        pltpu.make_async_copy(len_hbm, len_ref, nat_sem.at[3]),
    ]
    for cp in nat:
        cp.start()

    queries = ((q_hbm, qs), (do_hbm, dos))

    @pl.loop(0, heads)
    def _(h):
        for i, (src, dst) in enumerate(queries):
            pltpu.make_async_copy(
                src.at[:, cols(heads * core + h)], dst.at[h, half(core)], q_loc.at[i]
            ).start()

    for cp in nat:
        cp.wait()
    lane = lax.broadcasted_iota(jnp.int32, (rows, 4 * group), 1)
    delta = jnp.zeros((rows, 4 * group), F32)
    for h in range(4 * group):
        at = slice(h * HD, (h + 1) * HD)
        col = jnp.sum(o_nat[:, at].astype(F32) * do_nat[:, at].astype(F32), axis=1, keepdims=True)
        delta = jnp.where(lane == h, col, delta)
    norm = lse_ref[...].T * LOG2E
    first_half = core == 0
    for i, flip in ((0, False), (1, True)):
        low = jnp.logical_xor(first_half, flip)
        pd[i, :, :heads] = jnp.where(low, norm[:, :heads], norm[:, heads:])
        pd[i, :, heads : 2 * heads] = jnp.where(low, delta[:, :heads], delta[:, heads:])
    pl.semaphore_wait(barrier, len(partners))

    kinds = [(0, 0, 1, 1), (1, 1, 1, 7), (2, 0, 0, 0), (3, 1, 8, 0), (4, 0, 8, 8), (5, 1, 0, 8)]

    def first(kind, d, which, around=False):
        _, b, slot, hop = kinds[kind]
        to_core = core if d == 0 else other
        src = (k_hbm, v_hbm)[which].at[:, cols(2 * to_core + b)]
        dst = kv.at[b, slot, which, half(core)]
        if hop == 0 and d == 0:
            return pltpu.make_async_copy(src, dst, fh_recv.at[kind, core, which])
        if kind > 3 and around:
            dst, hop = relay.at[0, b, which, half(core)], -8
        return remote(src, dst, fh_send.at[kind, d, which], fh_recv.at[kind, core, which], hop, to_core)

    def start_first(kind):
        for which in (0, 1):
            for d in (0, 1):
                if kind > 3:
                    pl.when(place != 0)(lambda: first(kind, d, which).start())
                    pl.when(place == 0)(lambda: first(kind, d, which, True).start())
                else:
                    first(kind, d, which).start()

    def wait_first(kind, which, c):
        _, b, slot, hop = kinds[kind]
        dst = kv.at[b, slot, which, pl.ds(c * rows, rows)]
        pltpu.make_async_copy(dst, dst, fh_recv.at[kind, c, which]).wait()

    def piece(ref, b, t, which, r):
        return ref.at[b, t, which, pl.ds(r * rows, rows)]

    def ring(b, t, which, r):
        return remote(
            piece(kv, b, t, which, r), piece(kv, b, t + 1, which, r),
            ring_send.at[b, t, which, r], ring_recv.at[b, t + 1, which, r], 1 - 2 * b, core,
        )

    def first_arrives(which, r):
        for b in (0, 1):
            wait_first(b, which, r)
            ring(b, 1, which, r).start()

    start_first(0)
    start_first(1)

    pd_copy = remote(pd.at[1], pd.at[2], pd_send.at[0], pd_recv.at[0], 0, other)
    pd_copy.start()

    @pl.loop(0, heads)
    def _(h):
        for i, (src, dst) in enumerate(queries):
            remote(
                src.at[:, cols(heads * other + h)], dst.at[h, half(core)],
                q_send.at[i], q_recv.at[i], 0, other,
            ).start()

    for kind in (2, 5, 3, 4):
        start_first(kind)

    row = chip * block + lax.broadcasted_iota(jnp.int32, (block, HD), 0)
    low_key = jnp.zeros((block, HD), jnp.int32)
    end = jnp.int32(0)
    for d in range(len_ref.shape[0]):
        end = end + len_ref[d]
        low_key = jnp.where(row >= end, end, low_key)
    lo_ref[...] = low_key

    dqacc[...] = jnp.zeros_like(dqacc)
    for b in (0, 1):
        acc[b, 1] = jnp.zeros(acc.shape[2:], acc.dtype)

    first_arrives(0, 0)
    first_arrives(0, 1)
    for i, (dst, turned) in enumerate(((qs, qt), (dos, dot_t))):
        mine = dst.at[:, half(core)]
        theirs = dst.at[:, half(other)]
        pltpu.make_async_copy(mine, mine, q_loc.at[i]).wait()
        pltpu.make_async_copy(theirs, theirs, q_recv.at[i]).wait()
        for h in range(heads):
            turned[:, h * block : (h + 1) * block] = dst[h].T
        first_arrives(1, i)
    pd_copy.wait_recv()
    for i, at in ((0, core), (2, other)):
        for h in range(heads):
            lb[h, half(at)] = jnp.broadcast_to(pd[i, :, h : h + 1], (rows, HD))
            db[h, half(at)] = jnp.broadcast_to(pd[i, :, heads + h : heads + h + 1], (rows, HD))

    def pass_on(b, t, which, r):
        return remote(
            acc.at[b, t, which, r], acc.at[b, t + 1, which, r],
            acc_send.at[b, t, which, r], acc_recv.at[b, t + 1, which, r], 1 - 2 * b, core,
        )

    def go_home(b, which, r):
        return remote(
            acc.at[b, HOPS - 1, which, r], home.at[b, core, which],
            home_send.at[b, r, which], home_recv.at[b, core, which], -7 if b == 0 else -1, r,
        )

    def far_home(b, which, r):
        return remote(
            p8.at[b, which, r], h8.at[b, core, which],
            h8_send.at[b, r, which], h8_recv.at[b, core, which], -8, r,
        )

    def passing(stage, b, hop):
        src = relay.at[stage, b]
        dst = relay.at[1, b] if stage == 0 else kv.at[b, HOPS * (1 - b)]
        return remote(src, dst, relay_send.at[stage, b], relay_recv.at[stage, b], hop, core)

    def keys_stage(stage, b):
        @pl.when(place == 0)
        def _():
            if stage == 0:
                for which in (0, 1):
                    for c in (0, 1):
                        wait_first(4 + b, which, c)
            else:
                passing(0, b, -8).wait_recv()
            passing(stage, b, -8).start()

    def sums_out(stage, b):
        src = p8.at[b] if stage == 0 else sums.at[0, b]
        return remote(
            src, sums.at[stage, b], relay_send.at[stage, b], relay_recv.at[stage, b], 8, core
        )

    def sums_home(b, which, r):
        return remote(
            sums.at[1, b, which, r], h8.at[b, core, which],
            h8_send.at[b, r, which], h8_recv.at[b, core, which], 8, r,
        )

    def sums_stage(stage, b):
        @pl.when(place == HOPS - 1)
        def _():
            sums_out(stage - 1, b).wait_recv()
            if stage == 1:
                sums_out(1, b).start()
            else:
                for which in (0, 1):
                    for r in (0, 1):
                        sums_home(b, which, r).start()

    def own_home(b, which):
        return remote(
            pf.at[1, b, which, other], own.at[b, core, which],
            own_send.at[b, which], own_recv.at[b, which], 0, other,
        )

    step = group // 2

    def wide(x):
        return jnp.concatenate([x] * (block // HD), axis=-1) if block >= HD else x[..., :block]

    def chunk(b, slot, distance, to):
        keys = kv[b, slot, 0]
        values = kv[b, slot, 1]
        key_at = (chip - distance) * block + lax.broadcasted_iota(jnp.int32, (block, block), 1)
        row_at = chip * block + lax.broadcasted_iota(jnp.int32, (block, block), 0)
        bias = jnp.where((key_at >= wide(lo_ref[...])) & (key_at <= row_at), 0.0, MASKED)
        dk_t = jnp.zeros((HD, block), F32)
        dv_t = jnp.zeros((HD, block), F32)
        for h in range(b * group, (b + 1) * group, step):
            some = slice(h, h + step)
            flat = slice(h * block, (h + step) * block)
            q = qs[some].reshape(step * block, HD)
            g = dos[some].reshape(step * block, HD)
            s = dot(q, keys, NT).reshape(step, block, block)
            dp = dot(g, values, NT).reshape(step, block, block)
            p = jnp.exp2(s * (SCALE * LOG2E) - wide(lb[some]) + bias[None])
            ds = (p * (dp - wide(db[some]))).astype(BF).reshape(step * block, block)
            ph = p.astype(BF).reshape(step * block, block)
            dv_t = dv_t + dot(dot_t[:, flat], ph, NN)
            dk_t = dk_t + dot(qt[:, flat], ds, NN)
            dqacc[some] += dot(ds, keys, NN).reshape(step, block, HD)
        for which, part in enumerate((dk_t, dv_t)):
            for r in (0, 1):
                pf[to, b, which, r] = part[:, r * rows : (r + 1) * rows]

    def own_block(b):
        for which in (0, 1):
            for c in (0, 1):
                wait_first(2 + b, which, c)
        chunk(b, HOPS * b, 0, 1)
        for which in (0, 1):
            own_home(b, which).start()
            own[b, core, which] = pf[1, b, which, core]

    def far_block(b):
        @pl.when(place != 0)
        def _():
            for which in (0, 1):
                for c in (0, 1):
                    wait_first(4 + b, which, c)

        @pl.when(place == 0)
        def _():
            passing(1, b, -8).wait_recv()

        chunk(b, HOPS * (1 - b), HOPS, 2)
        p8[b] = pf[2, b].astype(BF)

        @pl.when(place != HOPS - 1)
        def _():
            for which in (0, 1):
                for r in (0, 1):
                    far_home(b, which, r).start()

        @pl.when(place == HOPS - 1)
        def _():
            sums_out(0, b).start()

    own_block(0)
    keys_stage(0, 0)

    @pl.loop(1, HOPS)
    def _(t):
        def arrives(which, r):
            @pl.when(t < HOPS - 1)
            def _():
                for b in (0, 1):
                    ring(b, t, which, r).wait_recv()

                    @pl.when(t < HOPS - 2)
                    def _():
                        ring(b, t + 1, which, r).start()

        def add(which):
            for r in (0, 1):
                for b in (0, 1):
                    @pl.when(t > 1)
                    def _():
                        pass_on(b, t - 1, which, r).wait_recv()

                    acc[b, t, which, r] = (acc[b, t, which, r].astype(F32) + pf[0, b, which, r]).astype(BF)

                    @pl.when(t < HOPS - 1)
                    def _():
                        pass_on(b, t, which, r).start()

                    @pl.when(t == HOPS - 1)
                    def _():
                        go_home(b, which, r).start()

        chunk(0, t, t, 0)
        arrives(0, 0)
        arrives(0, 1)
        chunk(1, t, HOPS - t, 0)
        arrives(1, 0)
        add(0)
        add(1)
        pl.when(t == 2)(lambda: own_block(1))
        pl.when(t == 3)(lambda: far_block(0))
        pl.when(t == 4)(lambda: far_block(1))
        arrives(1, 1)

        @pl.when(t == 1)
        def _():
            keys_stage(0, 1)
            keys_stage(1, 0)

        pl.when(t == 2)(lambda: keys_stage(1, 1))
        pl.when(t == 4)(lambda: sums_stage(1, 0))

        @pl.when(t == 5)
        def _():
            sums_stage(2, 0)
            sums_stage(1, 1)

        pl.when(t == 6)(lambda: sums_stage(2, 1))

    dqs[...] = (dqacc[...] * SCALE).astype(BF)

    @pl.loop(0, heads)
    def _(h):
        pltpu.make_async_copy(
            dqs.at[h, half(core)], dq_hbm.at[:, cols(heads * core + h)], dq_loc.at[0]
        ).start()
        remote(
            dqs.at[h, half(other)], dq_hbm.at[:, cols(heads * core + h)],
            dq_send.at[0], dq_recv.at[0], 0, other,
        ).start()

    for b in (0, 1):
        for which in (0, 1):
            got = own.at[b, other, which]
            pltpu.make_async_copy(got, got, own_recv.at[b, which]).wait()
            for c in (0, 1):
                for buf, sems in ((h8, h8_recv), (home, home_recv)):
                    got = buf.at[b, c, which]
                    pltpu.make_async_copy(got, got, sems.at[b, c, which]).wait()
    for c in (0, 1):
        for b in (0, 1):
            at = slice((2 * c + b) * HD, (2 * c + b + 1) * HD)
            total = [
                own[b, c, which] + h8[b, c, which].astype(F32) + home[b, c, which].astype(F32)
                for which in (0, 1)
            ]
            dk_ref[:, at] = (total[0] * SCALE).T.astype(BF)
            dv_ref[:, at] = total[1].T.astype(BF)

    for i, dst in enumerate((qs, dos)):
        out = dst.at[:, half(core)]
        pltpu.make_async_copy(out, out, q_send.at[i]).wait()
    pd_copy.wait_send()
    for kind in range(6):
        for which in (0, 1):
            for d in (0, 1):
                if not (kinds[kind][3] == 0 and d == 0):
                    first(kind, d, which).wait_send()
    @pl.when((place == 0) | (place == HOPS - 1))
    def _():
        for b in (0, 1):
            for stage in (0, 1):
                passing(stage, b, 8).wait_send()

    for b in (0, 1):
        for which in (0, 1):
            for r in (0, 1):
                far_home(b, which, r).wait_send()
                go_home(b, which, r).wait_send()
                for t in range(1, HOPS - 1):
                    ring(b, t, which, r).wait_send()
                    pass_on(b, t, which, r).wait_send()
            own_home(b, which).wait_send()
    out = dq_hbm.at[:, cols(heads * core, heads)]
    pltpu.make_async_copy(out, out, dq_loc.at[0]).wait()
    pltpu.make_async_copy(out, out, dq_send.at[0]).wait()
    got = dq_hbm.at[:, cols(heads * other, heads)]
    pltpu.make_async_copy(got, got, dq_recv.at[0]).wait()


def finish(dq, dk, dv, dq_out, dk_out, dv_out, sems):
    copies = [
        pltpu.make_async_copy(a, b, sems.at[i])
        for i, (a, b) in enumerate(((dq, dq_out), (dk, dk_out), (dv, dv_out)))
    ]
    for cp in copies:
        cp.start()
    for cp in copies:
        cp.wait()


def body(query_rows, key_rows, value_rows, fwd_output, grad_output, log_normalizer, doc_lengths):
    rows = query_rows.shape[0]
    group = query_rows.shape[1] // key_rows.shape[1]
    chips = lax.axis_size("ctx") * 2
    heads = 2 * group
    block = 2 * rows
    any_space = pl.BlockSpec(memory_space=pl.ANY)
    vmem = pl.BlockSpec(memory_space=pltpu.VMEM)
    dma = pltpu.SemaphoreType.DMA
    slots = HOPS + 1
    flops = 2 * slots * group * block * block * HD * 2 * 5
    grads = pl.pallas_call(
        functools.partial(kernel, chips, group, rows, None),
        out_shape=[
            pltpu.VMEM(query_rows.shape, BF),
            pltpu.VMEM(key_rows.shape, BF),
            pltpu.VMEM(value_rows.shape, BF),
        ],
        in_specs=[any_space] * 7,
        out_specs=[vmem, vmem, vmem],
        scratch_shapes=[
            pltpu.VMEM((2 * heads, rows), F32),
            pltpu.SMEM(doc_lengths.shape, jnp.int32),
            pltpu.VMEM((heads, block, HD), BF),
            pltpu.VMEM((heads, block, HD), BF),
            pltpu.VMEM((HD, heads * block), BF),
            pltpu.VMEM((HD, heads * block), BF),
            pltpu.VMEM((rows, 2 * heads * HD), BF),
            pltpu.VMEM((rows, 2 * heads * HD), BF),
            pltpu.VMEM((heads, block, HD), F32),
            pltpu.VMEM((heads, block, HD), F32),
            pltpu.VMEM((block, HD), jnp.int32),
            pltpu.VMEM((3, rows, HD), F32),
            pltpu.VMEM((heads, block, HD), F32),
            pltpu.VMEM((heads, block, HD), BF),
            pltpu.VMEM((2, slots, 2, block, HD), BF),
            pltpu.VMEM((2, HOPS, 2, 2, HD, rows), BF),
            pltpu.VMEM((3, 2, 2, 2, HD, rows), F32),
            pltpu.VMEM((2, 2, 2, HD, rows), BF),
            pltpu.VMEM((2, 2, 2, HD, rows), F32),
            pltpu.VMEM((2, 2, 2, HD, rows), BF),
            pltpu.VMEM((2, 2, 2, HD, rows), BF),
            pltpu.VMEM((2, 2, 2, block, HD), BF),
            pltpu.VMEM((2, 2, 2, 2, HD, rows), BF),
            dma((6, 2, 2)), dma((6, 2, 2)),
            dma((2, slots, 2, 2)), dma((2, slots, 2, 2)),
            dma((2, slots, 2, 2)), dma((2, slots, 2, 2)),
            dma((2, 2, 2)), dma((2, 2, 2)),
            dma((2, 2, 2)), dma((2, 2, 2)),
            dma((2, 2)), dma((2, 2)),
            dma((2, 2)), dma((2, 2)),
            dma((4,)), dma((2,)), dma((2,)), dma((2,)),
            dma((1,)), dma((1,)), dma((1,)), dma((1,)), dma((1,)),
        ],
        compiler_params=pltpu.CompilerParams(
            collective_id=0, has_side_effects=True, vmem_limit_bytes=48 * 2**20
        ),
        cost_estimate=pl.CostEstimate(
            flops=flops, bytes_accessed=8 * rows * 2 * heads * HD, transcendentals=flops // (10 * HD)
        ),
    )(
        *(
            pltpu.with_memory_space_constraint(x, pltpu.HBM)
            for x in (query_rows, key_rows, value_rows, fwd_output, grad_output, log_normalizer.T, doc_lengths)
        )
    )
    return pl.pallas_call(
        finish,
        out_shape=[jax.ShapeDtypeStruct(x.shape, x.dtype) for x in (query_rows, key_rows, value_rows)],
        in_specs=[vmem] * 3,
        out_specs=[any_space] * 3,
        scratch_shapes=[dma((3,))],
    )(*(pltpu.with_memory_space_constraint(x, pltpu.VMEM) for x in grads))


def solution(mesh):
    tokens = P(("dp", "ctx", "head"), None)
    return jax.shard_map(
        body,
        mesh=mesh,
        in_specs=(tokens,) * 6 + (P("dp"),),
        out_specs=(tokens,) * 3,
        check_vma=False,
    )
```

```python
import functools

import jax
import jax.numpy as jnp
from jax import lax
from jax.experimental import pallas as pl
from jax.experimental.pallas import tpu as pltpu
from jax.sharding import PartitionSpec as P

HD = 128
LOG2E = 1.4426950408889634
SCALE = HD ** (-0.5)
HOPS = 8
MASKED = -1e30
MESH = pl.DeviceIdType.MESH
NN = (((1,), (0,)), ((), ()))
NT = (((1,), (1,)), ((), ()))
BF = jnp.bfloat16
F32 = jnp.float32


def dot(a, b, dims):
    return lax.dot_general(a, b, dims, preferred_element_type=F32)


def kernel(
    chips, group, rows, parts,
    q_hbm, k_hbm, v_hbm, o_hbm, do_hbm, lse_hbm, len_hbm,
    dq_hbm, dk_ref, dv_ref,
    lse_ref, len_ref,
    qs, dos, qt, dot_t, o_nat, do_nat, lb, db, lo_ref, pd, dqacc, dqs,
    kv, acc, pf, p8, own, h8, home, relay, sums,
    fh_send, fh_recv, ring_send, ring_recv, acc_send, acc_recv,
    home_send, home_recv, h8_send, h8_recv, own_send, own_recv,
    relay_send, relay_recv, nat_sem, q_loc, q_send, q_recv, pd_send, pd_recv, dq_loc, dq_send, dq_recv,
):
    heads = 2 * group
    block = 2 * rows
    at_ctx, at_head = lax.axis_index("ctx"), lax.axis_index("head")
    core = lax.rem(at_head, 2)
    chip = at_ctx * 2 + lax.div(at_head, 2)
    other = 1 - core
    place = lax.rem(chip, HOPS)

    def device(hop, to_core):
        to = lax.rem(chip + hop + chips, chips)
        return {"ctx": lax.div(to, 2), "head": lax.rem(to, 2) * 2 + to_core}

    def remote(src, dst, ss, rs, hop, to_core):
        return pltpu.make_async_remote_copy(
            src_ref=src, dst_ref=dst, send_sem=ss, recv_sem=rs,
            device_id=device(hop, to_core), device_id_type=MESH,
        )

    def cols(head, width=1):
        return pl.ds(pl.multiple_of(head * HD, HD), width * HD)

    def half(which):
        return pl.ds(pl.multiple_of(which * rows, rows), rows)

    barrier = pltpu.get_barrier_semaphore()
    partners = [(0, other)] + [(h, c) for h in (1, -1, 7, -7, 8, -8) for c in (0, 1)]
    for hop, c in partners:
        pl.semaphore_signal(barrier, inc=1, device_id=device(hop, c), device_id_type=MESH)
    nat = [
        pltpu.make_async_copy(o_hbm, o_nat, nat_sem.at[0]),
        pltpu.make_async_copy(do_hbm, do_nat, nat_sem.at[1]),
        pltpu.make_async_copy(lse_hbm, lse_ref, nat_sem.at[2]),
        pltpu.make_async_copy(len_hbm, len_ref, nat_sem.at[3]),
    ]
    for cp in nat:
        cp.start()

    queries = ((q_hbm, qs), (do_hbm, dos))

    @pl.loop(0, heads)
    def _(h):
        for i, (src, dst) in enumerate(queries):
            pltpu.make_async_copy(
                src.at[:, cols(heads * core + h)], dst.at[h, half(core)], q_loc.at[i]
            ).start()

    for cp in nat:
        cp.wait()
    lane = lax.broadcasted_iota(jnp.int32, (rows, 4 * group), 1)
    delta = jnp.zeros((rows, 4 * group), F32)
    for h in range(4 * group):
        at = slice(h * HD, (h + 1) * HD)
        col = jnp.sum(o_nat[:, at].astype(F32) * do_nat[:, at].astype(F32), axis=1, keepdims=True)
        delta = jnp.where(lane == h, col, delta)
    norm = lse_ref[...].T * LOG2E
    first_half = core == 0
    for i, flip in ((0, False), (1, True)):
        low = jnp.logical_xor(first_half, flip)
        pd[i, :, :heads] = jnp.where(low, norm[:, :heads], norm[:, heads:])
        pd[i, :, heads : 2 * heads] = jnp.where(low, delta[:, :heads], delta[:, heads:])
    row = chip * block + lax.broadcasted_iota(jnp.int32, (block, HD), 0)
    low_key = jnp.zeros((block, HD), jnp.int32)
    end = jnp.int32(0)
    for d in range(len_ref.shape[0]):
        end = end + len_ref[d]
        low_key = jnp.where(row >= end, end, low_key)
    lo_ref[...] = low_key

    dqacc[...] = jnp.zeros_like(dqacc)
    for b in (0, 1):
        acc[b, 1] = jnp.zeros(acc.shape[2:], acc.dtype)
    pl.semaphore_wait(barrier, len(partners))

    kinds = [(0, 0, 1, 1), (1, 1, 1, 7), (2, 0, 0, 0), (3, 1, 8, 0), (4, 0, 8, 8), (5, 1, 0, 8)]

    def first(kind, d, which, around=False):
        _, b, slot, hop = kinds[kind]
        to_core = core if d == 0 else other
        src = (k_hbm, v_hbm)[which].at[:, cols(2 * to_core + b)]
        dst = kv.at[b, slot, which, half(core)]
        if hop == 0 and d == 0:
            return pltpu.make_async_copy(src, dst, fh_recv.at[kind, core, which])
        if kind > 3 and around:
            dst, hop = relay.at[0, b, which, half(core)], -8
        return remote(src, dst, fh_send.at[kind, d, which], fh_recv.at[kind, core, which], hop, to_core)

    def start_first(kind):
        for which in (0, 1):
            for d in (0, 1):
                if kind > 3:
                    pl.when(place != 0)(lambda: first(kind, d, which).start())
                    pl.when(place == 0)(lambda: first(kind, d, which, True).start())
                else:
                    first(kind, d, which).start()

    def wait_first(kind, which, c):
        _, b, slot, hop = kinds[kind]
        dst = kv.at[b, slot, which, pl.ds(c * rows, rows)]
        pltpu.make_async_copy(dst, dst, fh_recv.at[kind, c, which]).wait()

    def piece(ref, b, t, which, r):
        return ref.at[b, t, which, pl.ds(r * rows, rows)]

    def ring(b, t, which, r):
        return remote(
            piece(kv, b, t, which, r), piece(kv, b, t + 1, which, r),
            ring_send.at[b, t, which, r], ring_recv.at[b, t + 1, which, r], 1 - 2 * b, core,
        )

    def first_arrives(which, r):
        for b in (0, 1):
            wait_first(b, which, r)
            ring(b, 1, which, r).start()

    start_first(0)
    start_first(1)

    pd_copy = remote(pd.at[1], pd.at[2], pd_send.at[0], pd_recv.at[0], 0, other)
    pd_copy.start()

    @pl.loop(0, heads)
    def _(h):
        for i, (src, dst) in enumerate(queries):
            remote(
                src.at[:, cols(heads * other + h)], dst.at[h, half(core)],
                q_send.at[i], q_recv.at[i], 0, other,
            ).start()

    for kind in (2, 4, 3, 5):
        start_first(kind)

    first_arrives(0, 0)
    first_arrives(0, 1)
    for i, (dst, turned) in enumerate(((qs, qt), (dos, dot_t))):
        mine = dst.at[:, half(core)]
        theirs = dst.at[:, half(other)]
        pltpu.make_async_copy(mine, mine, q_loc.at[i]).wait()
        pltpu.make_async_copy(theirs, theirs, q_recv.at[i]).wait()
        for h in range(heads):
            turned[:, h * block : (h + 1) * block] = dst[h].T
        first_arrives(1, i)
    pd_copy.wait_recv()
    for i, at in ((0, core), (2, other)):
        for h in range(heads):
            lb[h, half(at)] = jnp.broadcast_to(pd[i, :, h : h + 1], (rows, HD))
            db[h, half(at)] = jnp.broadcast_to(pd[i, :, heads + h : heads + h + 1], (rows, HD))

    def pass_on(b, t, which, r):
        return remote(
            acc.at[b, t, which, r], acc.at[b, t + 1, which, r],
            acc_send.at[b, t, which, r], acc_recv.at[b, t + 1, which, r], 1 - 2 * b, core,
        )

    def go_home(b, which, r):
        return remote(
            acc.at[b, HOPS - 1, which, r], home.at[b, core, which],
            home_send.at[b, r, which], home_recv.at[b, core, which], -7 if b == 0 else -1, r,
        )

    def far_home(b, which, r):
        return remote(
            p8.at[b, which, r], h8.at[b, core, which],
            h8_send.at[b, r, which], h8_recv.at[b, core, which], -8, r,
        )

    def passing(stage, b, hop):
        src = relay.at[stage, b]
        dst = relay.at[1, b] if stage == 0 else kv.at[b, HOPS * (1 - b)]
        return remote(src, dst, relay_send.at[stage, b], relay_recv.at[stage, b], hop, core)

    def keys_stage(stage, b):
        @pl.when(place == 0)
        def _():
            if stage == 0:
                for which in (0, 1):
                    for c in (0, 1):
                        wait_first(4 + b, which, c)
            else:
                passing(0, b, -8).wait_recv()
            passing(stage, b, -8).start()

    def sums_out(stage, b):
        src = p8.at[b] if stage == 0 else sums.at[0, b]
        return remote(
            src, sums.at[stage, b], relay_send.at[stage, b], relay_recv.at[stage, b], 8, core
        )

    def sums_home(b, which, r):
        return remote(
            sums.at[1, b, which, r], h8.at[b, core, which],
            h8_send.at[b, r, which], h8_recv.at[b, core, which], 8, r,
        )

    def sums_stage(stage, b):
        @pl.when(place == HOPS - 1)
        def _():
            sums_out(stage - 1, b).wait_recv()
            if stage == 1:
                sums_out(1, b).start()
            else:
                for which in (0, 1):
                    for r in (0, 1):
                        sums_home(b, which, r).start()

    def own_home(b, which):
        return remote(
            pf.at[1, b, which, other], own.at[b, core, which],
            own_send.at[b, which], own_recv.at[b, which], 0, other,
        )

    step = group // 2

    def wide(x):
        return jnp.concatenate([x] * (block // HD), axis=-1) if block >= HD else x[..., :block]

    def chunk(b, slot, distance, to):
        keys = kv[b, slot, 0]
        values = kv[b, slot, 1]
        key_at = (chip - distance) * block + lax.broadcasted_iota(jnp.int32, (block, block), 1)
        row_at = chip * block + lax.broadcasted_iota(jnp.int32, (block, block), 0)
        bias = jnp.where((key_at >= wide(lo_ref[...])) & (key_at <= row_at), 0.0, MASKED)
        dk_t = jnp.zeros((HD, block), F32)
        dv_t = jnp.zeros((HD, block), F32)
        for h in range(b * group, (b + 1) * group, step):
            some = slice(h, h + step)
            flat = slice(h * block, (h + step) * block)
            q = qs[some].reshape(step * block, HD)
            g = dos[some].reshape(step * block, HD)
            s = dot(q, keys, NT).reshape(step, block, block)
            dp = dot(g, values, NT).reshape(step, block, block)
            p = jnp.exp2(s * (SCALE * LOG2E) - wide(lb[some]) + bias[None])
            ds = (p * (dp - wide(db[some]))).astype(BF).reshape(step * block, block)
            ph = p.astype(BF).reshape(step * block, block)
            dv_t = dv_t + dot(dot_t[:, flat], ph, NN)
            dk_t = dk_t + dot(qt[:, flat], ds, NN)
            dqacc[some] += dot(ds, keys, NN).reshape(step, block, HD)
        for which, part in enumerate((dk_t, dv_t)):
            for r in (0, 1):
                pf[to, b, which, r] = part[:, r * rows : (r + 1) * rows]

    def own_block(b):
        for which in (0, 1):
            for c in (0, 1):
                wait_first(2 + b, which, c)
        chunk(b, HOPS * b, 0, 1)
        for which in (0, 1):
            own_home(b, which).start()
            own[b, core, which] = pf[1, b, which, core]

    def far_block(b):
        @pl.when(place != 0)
        def _():
            for which in (0, 1):
                for c in (0, 1):
                    wait_first(4 + b, which, c)

        @pl.when(place == 0)
        def _():
            passing(1, b, -8).wait_recv()

        chunk(b, HOPS * (1 - b), HOPS, 2)
        p8[b] = pf[2, b].astype(BF)

        @pl.when(place != HOPS - 1)
        def _():
            for which in (0, 1):
                for r in (0, 1):
                    far_home(b, which, r).start()

        @pl.when(place == HOPS - 1)
        def _():
            sums_out(0, b).start()

    own_block(0)
    keys_stage(0, 0)

    @pl.loop(1, HOPS)
    def _(t):
        def arrives(which, r):
            @pl.when(t < HOPS - 1)
            def _():
                for b in (0, 1):
                    ring(b, t, which, r).wait_recv()

                    @pl.when(t < HOPS - 2)
                    def _():
                        ring(b, t + 1, which, r).start()

        def add(which):
            for r in (0, 1):
                for b in (0, 1):
                    @pl.when(t > 1)
                    def _():
                        pass_on(b, t - 1, which, r).wait_recv()

                    acc[b, t, which, r] = (acc[b, t, which, r].astype(F32) + pf[0, b, which, r]).astype(BF)

                    @pl.when(t < HOPS - 1)
                    def _():
                        pass_on(b, t, which, r).start()

                    @pl.when(t == HOPS - 1)
                    def _():
                        go_home(b, which, r).start()

        chunk(0, t, t, 0)
        arrives(0, 0)
        arrives(0, 1)
        chunk(1, t, HOPS - t, 0)
        arrives(1, 0)
        add(0)
        add(1)
        pl.when(t == 2)(lambda: own_block(1))
        pl.when(t == 3)(lambda: far_block(0))
        pl.when(t == 4)(lambda: far_block(1))
        arrives(1, 1)

        @pl.when(t == 1)
        def _():
            keys_stage(0, 1)
            keys_stage(1, 0)

        pl.when(t == 2)(lambda: keys_stage(1, 1))
        pl.when(t == 4)(lambda: sums_stage(1, 0))

        @pl.when(t == 5)
        def _():
            sums_stage(1, 1)
            sums_stage(2, 0)

        pl.when(t == HOPS - 1)(lambda: sums_stage(2, 1))

    dqs[...] = (dqacc[...] * SCALE).astype(BF)

    @pl.loop(0, heads)
    def _(h):
        pltpu.make_async_copy(
            dqs.at[h, half(core)], dq_hbm.at[:, cols(heads * core + h)], dq_loc.at[0]
        ).start()
        remote(
            dqs.at[h, half(other)], dq_hbm.at[:, cols(heads * core + h)],
            dq_send.at[0], dq_recv.at[0], 0, other,
        ).start()

    for b in (0, 1):
        for which in (0, 1):
            got = own.at[b, other, which]
            pltpu.make_async_copy(got, got, own_recv.at[b, which]).wait()
            for c in (0, 1):
                for buf, sems in ((h8, h8_recv), (home, home_recv)):
                    got = buf.at[b, c, which]
                    pltpu.make_async_copy(got, got, sems.at[b, c, which]).wait()
    for c in (0, 1):
        for b in (0, 1):
            at = slice((2 * c + b) * HD, (2 * c + b + 1) * HD)
            total = [
                own[b, c, which] + h8[b, c, which].astype(F32) + home[b, c, which].astype(F32)
                for which in (0, 1)
            ]
            dk_ref[:, at] = (total[0] * SCALE).T.astype(BF)
            dv_ref[:, at] = total[1].T.astype(BF)

    for i, dst in enumerate((qs, dos)):
        out = dst.at[:, half(core)]
        pltpu.make_async_copy(out, out, q_send.at[i]).wait()
    pd_copy.wait_send()
    for kind in range(6):
        for which in (0, 1):
            for d in (0, 1):
                if not (kinds[kind][3] == 0 and d == 0):
                    first(kind, d, which).wait_send()
    @pl.when((place == 0) | (place == HOPS - 1))
    def _():
        for b in (0, 1):
            for stage in (0, 1):
                passing(stage, b, 8).wait_send()

    for b in (0, 1):
        for which in (0, 1):
            for r in (0, 1):
                far_home(b, which, r).wait_send()
                go_home(b, which, r).wait_send()
                for t in range(1, HOPS - 1):
                    ring(b, t, which, r).wait_send()
                    pass_on(b, t, which, r).wait_send()
            own_home(b, which).wait_send()
    out = dq_hbm.at[:, cols(heads * core, heads)]
    pltpu.make_async_copy(out, out, dq_loc.at[0]).wait()
    pltpu.make_async_copy(out, out, dq_send.at[0]).wait()
    got = dq_hbm.at[:, cols(heads * other, heads)]
    pltpu.make_async_copy(got, got, dq_recv.at[0]).wait()


def finish(dq, dk, dv, dq_out, dk_out, dv_out, sems):
    copies = [
        pltpu.make_async_copy(a, b, sems.at[i])
        for i, (a, b) in enumerate(((dq, dq_out), (dk, dk_out), (dv, dv_out)))
    ]
    for cp in copies:
        cp.start()
    for cp in copies:
        cp.wait()


def body(query_rows, key_rows, value_rows, fwd_output, grad_output, log_normalizer, doc_lengths):
    rows = query_rows.shape[0]
    group = query_rows.shape[1] // key_rows.shape[1]
    chips = lax.axis_size("ctx") * 2
    heads = 2 * group
    block = 2 * rows
    any_space = pl.BlockSpec(memory_space=pl.ANY)
    vmem = pl.BlockSpec(memory_space=pltpu.VMEM)
    dma = pltpu.SemaphoreType.DMA
    slots = HOPS + 1
    flops = 2 * slots * group * block * block * HD * 2 * 5
    grads = pl.pallas_call(
        functools.partial(kernel, chips, group, rows, None),
        out_shape=[
            pltpu.VMEM(query_rows.shape, BF),
            pltpu.VMEM(key_rows.shape, BF),
            pltpu.VMEM(value_rows.shape, BF),
        ],
        in_specs=[any_space] * 7,
        out_specs=[vmem, vmem, vmem],
        scratch_shapes=[
            pltpu.VMEM((2 * heads, rows), F32),
            pltpu.SMEM(doc_lengths.shape, jnp.int32),
            pltpu.VMEM((heads, block, HD), BF),
            pltpu.VMEM((heads, block, HD), BF),
            pltpu.VMEM((HD, heads * block), BF),
            pltpu.VMEM((HD, heads * block), BF),
            pltpu.VMEM((rows, 2 * heads * HD), BF),
            pltpu.VMEM((rows, 2 * heads * HD), BF),
            pltpu.VMEM((heads, block, HD), F32),
            pltpu.VMEM((heads, block, HD), F32),
            pltpu.VMEM((block, HD), jnp.int32),
            pltpu.VMEM((3, rows, HD), F32),
            pltpu.VMEM((heads, block, HD), F32),
            pltpu.VMEM((heads, block, HD), BF),
            pltpu.VMEM((2, slots, 2, block, HD), BF),
            pltpu.VMEM((2, HOPS, 2, 2, HD, rows), BF),
            pltpu.VMEM((3, 2, 2, 2, HD, rows), F32),
            pltpu.VMEM((2, 2, 2, HD, rows), BF),
            pltpu.VMEM((2, 2, 2, HD, rows), F32),
            pltpu.VMEM((2, 2, 2, HD, rows), BF),
            pltpu.VMEM((2, 2, 2, HD, rows), BF),
            pltpu.VMEM((2, 2, 2, block, HD), BF),
            pltpu.VMEM((2, 2, 2, 2, HD, rows), BF),
            dma((6, 2, 2)), dma((6, 2, 2)),
            dma((2, slots, 2, 2)), dma((2, slots, 2, 2)),
            dma((2, slots, 2, 2)), dma((2, slots, 2, 2)),
            dma((2, 2, 2)), dma((2, 2, 2)),
            dma((2, 2, 2)), dma((2, 2, 2)),
            dma((2, 2)), dma((2, 2)),
            dma((2, 2)), dma((2, 2)),
            dma((4,)), dma((2,)), dma((2,)), dma((2,)),
            dma((1,)), dma((1,)), dma((1,)), dma((1,)), dma((1,)),
        ],
        compiler_params=pltpu.CompilerParams(
            collective_id=0, has_side_effects=True, vmem_limit_bytes=48 * 2**20
        ),
        cost_estimate=pl.CostEstimate(
            flops=flops, bytes_accessed=8 * rows * 2 * heads * HD, transcendentals=flops // (10 * HD)
        ),
    )(
        *(
            pltpu.with_memory_space_constraint(x, pltpu.HBM)
            for x in (query_rows, key_rows, value_rows, fwd_output, grad_output, log_normalizer.T, doc_lengths)
        )
    )
    return pl.pallas_call(
        finish,
        out_shape=[jax.ShapeDtypeStruct(x.shape, x.dtype) for x in (query_rows, key_rows, value_rows)],
        in_specs=[vmem] * 3,
        out_specs=[any_space] * 3,
        scratch_shapes=[dma((3,))],
    )(*(pltpu.with_memory_space_constraint(x, pltpu.VMEM) for x in grads))


def solution(mesh):
    tokens = P(("dp", "ctx", "head"), None)
    return jax.shard_map(
        body,
        mesh=mesh,
        in_specs=(tokens,) * 6 + (P("dp"),),
        out_specs=(tokens,) * 3,
        check_vma=False,
    )
```

```python
import functools

import jax
import jax.numpy as jnp
from jax import lax
from jax.experimental import pallas as pl
from jax.experimental.pallas import tpu as pltpu
from jax.sharding import PartitionSpec as P

HD = 128
LOG2E = 1.4426950408889634
SCALE = HD ** (-0.5)
HOPS = 8
MASKED = -1e30
MESH = pl.DeviceIdType.MESH
NN = (((1,), (0,)), ((), ()))
NT = (((1,), (1,)), ((), ()))
BF = jnp.bfloat16
F32 = jnp.float32


def dot(a, b, dims):
    return lax.dot_general(a, b, dims, preferred_element_type=F32)


def kernel(
    chips, group, rows, parts,
    q_hbm, k_hbm, v_hbm, o_hbm, do_hbm, lse_hbm, len_hbm,
    dq_hbm, dk_ref, dv_ref,
    lse_ref, len_ref,
    qs, dos, qt, dot_t, o_nat, do_nat, lb, db, lo_ref, pd, dqacc, dqs,
    kv, acc, pf, p8, own, h8, home, relay, sums,
    fh_send, fh_recv, ring_send, ring_recv, acc_send, acc_recv,
    home_send, home_recv, h8_send, h8_recv, own_send, own_recv,
    relay_send, relay_recv, nat_sem, q_loc, q_send, q_recv, pd_send, pd_recv, dq_loc, dq_send, dq_recv,
):
    heads = 2 * group
    block = 2 * rows
    at_ctx, at_head = lax.axis_index("ctx"), lax.axis_index("head")
    core = lax.rem(at_head, 2)
    chip = at_ctx * 2 + lax.div(at_head, 2)
    other = 1 - core
    place = lax.rem(chip, HOPS)

    def device(hop, to_core):
        to = lax.rem(chip + hop + chips, chips)
        return {"ctx": lax.div(to, 2), "head": lax.rem(to, 2) * 2 + to_core}

    def remote(src, dst, ss, rs, hop, to_core):
        return pltpu.make_async_remote_copy(
            src_ref=src, dst_ref=dst, send_sem=ss, recv_sem=rs,
            device_id=device(hop, to_core), device_id_type=MESH,
        )

    def cols(head, width=1):
        return pl.ds(pl.multiple_of(head * HD, HD), width * HD)

    def half(which):
        return pl.ds(pl.multiple_of(which * rows, rows), rows)

    barrier = pltpu.get_barrier_semaphore()
    partners = [(0, other)] + [(h, c) for h in (1, -1, 7, -7, 8, -8) for c in (0, 1)]
    for hop, c in partners:
        pl.semaphore_signal(barrier, inc=1, device_id=device(hop, c), device_id_type=MESH)
    nat = [
        pltpu.make_async_copy(o_hbm, o_nat, nat_sem.at[0]),
        pltpu.make_async_copy(do_hbm, do_nat, nat_sem.at[1]),
        pltpu.make_async_copy(lse_hbm, lse_ref, nat_sem.at[2]),
        pltpu.make_async_copy(len_hbm, len_ref, nat_sem.at[3]),
    ]
    for cp in nat:
        cp.start()

    queries = ((q_hbm, qs), (do_hbm, dos))

    @pl.loop(0, heads)
    def _(h):
        for i, (src, dst) in enumerate(queries):
            pltpu.make_async_copy(
                src.at[:, cols(heads * core + h)], dst.at[h, half(core)], q_loc.at[i]
            ).start()

    for cp in nat:
        cp.wait()
    lane = lax.broadcasted_iota(jnp.int32, (rows, 4 * group), 1)
    delta = jnp.zeros((rows, 4 * group), F32)
    for h in range(4 * group):
        at = slice(h * HD, (h + 1) * HD)
        col = jnp.sum(o_nat[:, at].astype(F32) * do_nat[:, at].astype(F32), axis=1, keepdims=True)
        delta = jnp.where(lane == h, col, delta)
    norm = lse_ref[...].T * LOG2E
    first_half = core == 0
    for i, flip in ((0, False), (1, True)):
        low = jnp.logical_xor(first_half, flip)
        pd[i, :, :heads] = jnp.where(low, norm[:, :heads], norm[:, heads:])
        pd[i, :, heads : 2 * heads] = jnp.where(low, delta[:, :heads], delta[:, heads:])
    row = chip * block + lax.broadcasted_iota(jnp.int32, (block, HD), 0)
    low_key = jnp.zeros((block, HD), jnp.int32)
    end = jnp.int32(0)
    for d in range(len_ref.shape[0]):
        end = end + len_ref[d]
        low_key = jnp.where(row >= end, end, low_key)
    lo_ref[...] = low_key

    dqacc[...] = jnp.zeros_like(dqacc)
    for b in (0, 1):
        acc[b, 1] = jnp.zeros(acc.shape[2:], acc.dtype)
    pl.semaphore_wait(barrier, len(partners))

    kinds = [(0, 0, 1, 1), (1, 1, 1, 7), (2, 0, 0, 0), (3, 1, 8, 0), (4, 0, 8, 8), (5, 1, 0, 8)]

    def first(kind, d, which, around=False):
        _, b, slot, hop = kinds[kind]
        to_core = core if d == 0 else other
        src = (k_hbm, v_hbm)[which].at[:, cols(2 * to_core + b)]
        dst = kv.at[b, slot, which, half(core)]
        if hop == 0 and d == 0:
            return pltpu.make_async_copy(src, dst, fh_recv.at[kind, core, which])
        if kind > 3 and around:
            dst, hop = relay.at[0, b, which, half(core)], -8
        return remote(src, dst, fh_send.at[kind, d, which], fh_recv.at[kind, core, which], hop, to_core)

    def start_first(kind):
        for which in (0, 1):
            for d in (0, 1):
                if kind > 3:
                    pl.when(place != 0)(lambda: first(kind, d, which).start())
                    pl.when(place == 0)(lambda: first(kind, d, which, True).start())
                else:
                    first(kind, d, which).start()

    def wait_first(kind, which, c):
        _, b, slot, hop = kinds[kind]
        dst = kv.at[b, slot, which, pl.ds(c * rows, rows)]
        pltpu.make_async_copy(dst, dst, fh_recv.at[kind, c, which]).wait()

    def piece(ref, b, t, which, r):
        return ref.at[b, t, which, pl.ds(r * rows, rows)]

    def ring(b, t, which, r):
        return remote(
            piece(kv, b, t, which, r), piece(kv, b, t + 1, which, r),
            ring_send.at[b, t, which, r], ring_recv.at[b, t + 1, which, r], 1 - 2 * b, core,
        )

    def first_arrives(which, r):
        for b in (0, 1):
            wait_first(b, which, r)
            ring(b, 1, which, r).start()

    start_first(0)
    start_first(1)

    pd_copy = remote(pd.at[1], pd.at[2], pd_send.at[0], pd_recv.at[0], 0, other)
    pd_copy.start()

    @pl.loop(0, heads)
    def _(h):
        for i, (src, dst) in enumerate(queries):
            remote(
                src.at[:, cols(heads * other + h)], dst.at[h, half(core)],
                q_send.at[i], q_recv.at[i], 0, other,
            ).start()

    for kind in (2, 4, 3, 5):
        start_first(kind)

    first_arrives(0, 0)
    first_arrives(0, 1)
    for i, (dst, turned) in enumerate(((qs, qt), (dos, dot_t))):
        mine = dst.at[:, half(core)]
        theirs = dst.at[:, half(other)]
        pltpu.make_async_copy(mine, mine, q_loc.at[i]).wait()
        pltpu.make_async_copy(theirs, theirs, q_recv.at[i]).wait()
        for h in range(heads):
            turned[:, h * block : (h + 1) * block] = dst[h].T
        first_arrives(1, i)
    pd_copy.wait_recv()
    for i, at in ((0, core), (2, other)):
        for h in range(heads):
            lb[h, half(at)] = jnp.broadcast_to(pd[i, :, h : h + 1], (rows, HD))
            db[h, half(at)] = jnp.broadcast_to(pd[i, :, heads + h : heads + h + 1], (rows, HD))

    def pass_on(b, t, which, r):
        return remote(
            acc.at[b, t, which, r], acc.at[b, t + 1, which, r],
            acc_send.at[b, t, which, r], acc_recv.at[b, t + 1, which, r], 1 - 2 * b, core,
        )

    def go_home(b, which, r):
        return remote(
            acc.at[b, HOPS - 1, which, r], home.at[b, core, which],
            home_send.at[b, r, which], home_recv.at[b, core, which], -7 if b == 0 else -1, r,
        )

    def far_home(b, which, r):
        return remote(
            p8.at[b, which, r], h8.at[b, core, which],
            h8_send.at[b, r, which], h8_recv.at[b, core, which], -8, r,
        )

    def passing(stage, b, hop):
        src = relay.at[stage, b]
        dst = relay.at[1, b] if stage == 0 else kv.at[b, HOPS * (1 - b)]
        return remote(src, dst, relay_send.at[stage, b], relay_recv.at[stage, b], hop, core)

    def keys_stage(stage, b):
        @pl.when(place == 0)
        def _():
            if stage == 0:
                for which in (0, 1):
                    for c in (0, 1):
                        wait_first(4 + b, which, c)
            else:
                passing(0, b, -8).wait_recv()
            passing(stage, b, -8).start()

    def sums_out(stage, b):
        src = p8.at[b] if stage == 0 else sums.at[0, b]
        return remote(
            src, sums.at[stage, b], relay_send.at[stage, b], relay_recv.at[stage, b], 8, core
        )

    def sums_home(b, which, r):
        return remote(
            sums.at[1, b, which, r], h8.at[b, core, which],
            h8_send.at[b, r, which], h8_recv.at[b, core, which], 8, r,
        )

    def sums_stage(stage, b):
        @pl.when(place == HOPS - 1)
        def _():
            sums_out(stage - 1, b).wait_recv()
            if stage == 1:
                sums_out(1, b).start()
            else:
                for which in (0, 1):
                    for r in (0, 1):
                        sums_home(b, which, r).start()

    def own_home(b, which):
        return remote(
            pf.at[1, b, which, other], own.at[b, core, which],
            own_send.at[b, which], own_recv.at[b, which], 0, other,
        )

    step = group

    def wide(x):
        return jnp.concatenate([x] * (block // HD), axis=-1) if block >= HD else x[..., :block]

    def chunk(b, slot, distance, to):
        keys = kv[b, slot, 0]
        values = kv[b, slot, 1]
        key_at = (chip - distance) * block + lax.broadcasted_iota(jnp.int32, (block, block), 1)
        row_at = chip * block + lax.broadcasted_iota(jnp.int32, (block, block), 0)
        bias = jnp.where((key_at >= wide(lo_ref[...])) & (key_at <= row_at), 0.0, MASKED)
        dk_t = jnp.zeros((HD, block), F32)
        dv_t = jnp.zeros((HD, block), F32)
        for h in range(b * group, (b + 1) * group, step):
            some = slice(h, h + step)
            flat = slice(h * block, (h + step) * block)
            q = qs[some].reshape(step * block, HD)
            g = dos[some].reshape(step * block, HD)
            s = dot(q, keys, NT).reshape(step, block, block)
            dp = dot(g, values, NT).reshape(step, block, block)
            p = jnp.exp2(s * (SCALE * LOG2E) - wide(lb[some]) + bias[None])
            ds = (p * (dp - wide(db[some]))).astype(BF).reshape(step * block, block)
            ph = p.astype(BF).reshape(step * block, block)
            dv_t = dv_t + dot(dot_t[:, flat], ph, NN)
            dk_t = dk_t + dot(qt[:, flat], ds, NN)
            dqacc[some] += dot(ds, keys, NN).reshape(step, block, HD)
        for which, part in enumerate((dk_t, dv_t)):
            for r in (0, 1):
                pf[to, b, which, r] = part[:, r * rows : (r + 1) * rows]

    def own_block(b):
        for which in (0, 1):
            for c in (0, 1):
                wait_first(2 + b, which, c)
        chunk(b, HOPS * b, 0, 1)
        for which in (0, 1):
            own_home(b, which).start()
            own[b, core, which] = pf[1, b, which, core]

    def far_block(b):
        @pl.when(place != 0)
        def _():
            for which in (0, 1):
                for c in (0, 1):
                    wait_first(4 + b, which, c)

        @pl.when(place == 0)
        def _():
            passing(1, b, -8).wait_recv()

        chunk(b, HOPS * (1 - b), HOPS, 2)
        p8[b] = pf[2, b].astype(BF)

        @pl.when(place != HOPS - 1)
        def _():
            for which in (0, 1):
                for r in (0, 1):
                    far_home(b, which, r).start()

        @pl.when(place == HOPS - 1)
        def _():
            sums_out(0, b).start()

    own_block(0)
    keys_stage(0, 0)

    @pl.loop(1, HOPS)
    def _(t):
        def arrives(which, r):
            @pl.when(t < HOPS - 1)
            def _():
                for b in (0, 1):
                    ring(b, t, which, r).wait_recv()

                    @pl.when(t < HOPS - 2)
                    def _():
                        ring(b, t + 1, which, r).start()

        def add(which):
            for r in (0, 1):
                for b in (0, 1):
                    @pl.when(t > 1)
                    def _():
                        pass_on(b, t - 1, which, r).wait_recv()

                    acc[b, t, which, r] = (acc[b, t, which, r].astype(F32) + pf[0, b, which, r]).astype(BF)

                    @pl.when(t < HOPS - 1)
                    def _():
                        pass_on(b, t, which, r).start()

                    @pl.when(t == HOPS - 1)
                    def _():
                        go_home(b, which, r).start()

        chunk(0, t, t, 0)
        arrives(0, 0)
        arrives(0, 1)
        chunk(1, t, HOPS - t, 0)
        arrives(1, 0)
        add(0)
        pl.when(t == 2)(lambda: own_block(1))
        pl.when(t == 3)(lambda: far_block(0))
        pl.when(t == 4)(lambda: far_block(1))
        add(1)
        arrives(1, 1)

        @pl.when(t == 1)
        def _():
            keys_stage(0, 1)
            keys_stage(1, 0)

        pl.when(t == 2)(lambda: keys_stage(1, 1))
        pl.when(t == 4)(lambda: sums_stage(1, 0))

        @pl.when(t == 5)
        def _():
            sums_stage(1, 1)
            sums_stage(2, 0)

        pl.when(t == HOPS - 1)(lambda: sums_stage(2, 1))

    dqs[...] = (dqacc[...] * SCALE).astype(BF)

    @pl.loop(0, heads)
    def _(h):
        pltpu.make_async_copy(
            dqs.at[h, half(core)], dq_hbm.at[:, cols(heads * core + h)], dq_loc.at[0]
        ).start()
        remote(
            dqs.at[h, half(other)], dq_hbm.at[:, cols(heads * core + h)],
            dq_send.at[0], dq_recv.at[0], 0, other,
        ).start()

    for i, dst in enumerate((qs, dos)):
        out = dst.at[:, half(core)]
        pltpu.make_async_copy(out, out, q_send.at[i]).wait()
    pd_copy.wait_send()
    for kind in range(6):
        for which in (0, 1):
            for d in (0, 1):
                if not (kinds[kind][3] == 0 and d == 0):
                    first(kind, d, which).wait_send()

    @pl.when((place == 0) | (place == HOPS - 1))
    def _():
        for b in (0, 1):
            for stage in (0, 1):
                passing(stage, b, 8).wait_send()

    for b in (0, 1):
        for which in (0, 1):
            for r in (0, 1):
                for t in range(1, HOPS - 1):
                    ring(b, t, which, r).wait_send()
                    pass_on(b, t, which, r).wait_send()
            own_home(b, which).wait_send()

    for b in (0, 1):
        for which in (0, 1):
            got = own.at[b, other, which]
            pltpu.make_async_copy(got, got, own_recv.at[b, which]).wait()
    for which in (0, 1):
        for b in (0, 1):
            for c in (0, 1):
                for buf, sems in ((h8, h8_recv), (home, home_recv)):
                    got = buf.at[b, c, which]
                    pltpu.make_async_copy(got, got, sems.at[b, c, which]).wait()
                at = slice((2 * c + b) * HD, (2 * c + b + 1) * HD)
                total = own[b, c, which] + h8[b, c, which].astype(F32) + home[b, c, which].astype(F32)
                if which == 0:
                    dk_ref[:, at] = (total * SCALE).T.astype(BF)
                else:
                    dv_ref[:, at] = total.T.astype(BF)

    for b in (0, 1):
        for which in (0, 1):
            for r in (0, 1):
                far_home(b, which, r).wait_send()
                go_home(b, which, r).wait_send()
    out = dq_hbm.at[:, cols(heads * core, heads)]
    pltpu.make_async_copy(out, out, dq_loc.at[0]).wait()
    pltpu.make_async_copy(out, out, dq_send.at[0]).wait()
    got = dq_hbm.at[:, cols(heads * other, heads)]
    pltpu.make_async_copy(got, got, dq_recv.at[0]).wait()


def finish(dq, dk, dv, dq_out, dk_out, dv_out, sems):
    copies = [
        pltpu.make_async_copy(a, b, sems.at[i])
        for i, (a, b) in enumerate(((dq, dq_out), (dk, dk_out), (dv, dv_out)))
    ]
    for cp in copies:
        cp.start()
    for cp in copies:
        cp.wait()


def body(query_rows, key_rows, value_rows, fwd_output, grad_output, log_normalizer, doc_lengths):
    rows = query_rows.shape[0]
    group = query_rows.shape[1] // key_rows.shape[1]
    chips = lax.axis_size("ctx") * 2
    heads = 2 * group
    block = 2 * rows
    any_space = pl.BlockSpec(memory_space=pl.ANY)
    vmem = pl.BlockSpec(memory_space=pltpu.VMEM)
    dma = pltpu.SemaphoreType.DMA
    slots = HOPS + 1
    flops = 2 * slots * group * block * block * HD * 2 * 5
    grads = pl.pallas_call(
        functools.partial(kernel, chips, group, rows, None),
        out_shape=[
            pltpu.VMEM(query_rows.shape, BF),
            pltpu.VMEM(key_rows.shape, BF),
            pltpu.VMEM(value_rows.shape, BF),
        ],
        in_specs=[any_space] * 7,
        out_specs=[vmem, vmem, vmem],
        scratch_shapes=[
            pltpu.VMEM((2 * heads, rows), F32),
            pltpu.SMEM(doc_lengths.shape, jnp.int32),
            pltpu.VMEM((heads, block, HD), BF),
            pltpu.VMEM((heads, block, HD), BF),
            pltpu.VMEM((HD, heads * block), BF),
            pltpu.VMEM((HD, heads * block), BF),
            pltpu.VMEM((rows, 2 * heads * HD), BF),
            pltpu.VMEM((rows, 2 * heads * HD), BF),
            pltpu.VMEM((heads, block, HD), F32),
            pltpu.VMEM((heads, block, HD), F32),
            pltpu.VMEM((block, HD), jnp.int32),
            pltpu.VMEM((3, rows, HD), F32),
            pltpu.VMEM((heads, block, HD), F32),
            pltpu.VMEM((heads, block, HD), BF),
            pltpu.VMEM((2, slots, 2, block, HD), BF),
            pltpu.VMEM((2, HOPS, 2, 2, HD, rows), BF),
            pltpu.VMEM((3, 2, 2, 2, HD, rows), F32),
            pltpu.VMEM((2, 2, 2, HD, rows), BF),
            pltpu.VMEM((2, 2, 2, HD, rows), F32),
            pltpu.VMEM((2, 2, 2, HD, rows), BF),
            pltpu.VMEM((2, 2, 2, HD, rows), BF),
            pltpu.VMEM((2, 2, 2, block, HD), BF),
            pltpu.VMEM((2, 2, 2, 2, HD, rows), BF),
            dma((6, 2, 2)), dma((6, 2, 2)),
            dma((2, slots, 2, 2)), dma((2, slots, 2, 2)),
            dma((2, slots, 2, 2)), dma((2, slots, 2, 2)),
            dma((2, 2, 2)), dma((2, 2, 2)),
            dma((2, 2, 2)), dma((2, 2, 2)),
            dma((2, 2)), dma((2, 2)),
            dma((2, 2)), dma((2, 2)),
            dma((4,)), dma((2,)), dma((2,)), dma((2,)),
            dma((1,)), dma((1,)), dma((1,)), dma((1,)), dma((1,)),
        ],
        compiler_params=pltpu.CompilerParams(
            collective_id=0, has_side_effects=True, vmem_limit_bytes=48 * 2**20
        ),
        cost_estimate=pl.CostEstimate(
            flops=flops, bytes_accessed=8 * rows * 2 * heads * HD, transcendentals=flops // (10 * HD)
        ),
    )(
        *(
            pltpu.with_memory_space_constraint(x, pltpu.HBM)
            for x in (query_rows, key_rows, value_rows, fwd_output, grad_output, log_normalizer.T, doc_lengths)
        )
    )
    return pl.pallas_call(
        finish,
        out_shape=[jax.ShapeDtypeStruct(x.shape, x.dtype) for x in (query_rows, key_rows, value_rows)],
        in_specs=[vmem] * 3,
        out_specs=[any_space] * 3,
        scratch_shapes=[dma((3,))],
    )(*(pltpu.with_memory_space_constraint(x, pltpu.VMEM) for x in grads))


def solution(mesh):
    tokens = P(("dp", "ctx", "head"), None)
    return jax.shard_map(
        body,
        mesh=mesh,
        in_specs=(tokens,) * 6 + (P("dp"),),
        out_specs=(tokens,) * 3,
        check_vma=False,
    )
```
